512 devices in a mesh: row: 16 (over z, x_lo), col: 32 (over y, x_hi, core).
Axes of the slice: x: 4 (x_hi: 2, x_lo: 2; x = x_hi * 2 + x_lo), y: 8, z: 8, core: 2. Of those that a mesh axis runs over, the one named last changes fastest.
Arguments:
- weights: bfloat16 [8192, 8192], P('row', 'col'), may hold values from -32 to 32, as said below
Outputs:
- edge_cycles: float32 [8192, 8192], P('row', 'col')
- account_cycles: float32 [8192], P(('row', 'col'))
The draws below stay inside these ranges and needn't reach their ends.
Inputs may be any that keep to these rules, and one draw needn't show every extreme that they name: `weights`: about half of the entries are zero.
All inputs are finite; a program needn't handle non-finite values.
Results may differ from the reference program's by a relative error of at most 0.0003.
Values may be sent and summed in bfloat16 or wider, within the bound.
A program may use at most 64 MiB of HBM per device.

```python
import math
import jax
import jax.numpy as jnp
from jax import lax

N = 8192


def draw_weights(key, part):
    key = jax.random.fold_in(key, 1)
    keys = jax.random.split(key, 4)
    occupied = jax.random.bernoulli(keys[0], 0.5, (N, N))
    values = jnp.clip(jax.random.normal(keys[1], (N, N), jnp.float32), -4.0, 4.0)
    lower, upper = (0.5, 2.0)
    row_scale = jnp.exp(jax.random.uniform(keys[2], (N,), jnp.float32, jnp.log(lower), jnp.log(upper)))
    col_scale = jnp.exp(jax.random.uniform(keys[3], (N,), jnp.float32, jnp.log(lower), jnp.log(upper)))
    result = jnp.where(occupied, values, 0.0) * row_scale[:, None] * col_scale[None, :]
    return result.astype(jnp.bfloat16)


def setup_inputs(seed: int = 0) -> dict:
    key_list = jax.random.split(jax.random.key(seed), 2)
    weights = draw_weights(jax.random.fold_in(key_list[1], 71), 0)
    return {"weights": weights}


def reference(weights):
    paths = jnp.dot(weights, weights, preferred_element_type=jnp.float32)
    edge_cycles = paths * weights.T.astype(jnp.float32) * (2.0 / math.sqrt(N))
    account_cycles = lax.optimization_barrier(jnp.sum(edge_cycles, axis=1)) / math.sqrt(N)
    return (edge_cycles, account_cycles)
```

```python
import math

import jax
import jax.numpy as jnp
from jax import lax
from jax.experimental import pallas as pl
from jax.experimental.pallas import tpu as pltpu
from jax.sharding import PartitionSpec as P

MESH = pl.DeviceIdType.MESH
PHASES = 4


def kernel(
    w_ref, edge_ref, acct_ref,
    a_buf, b_buf, part, inbox, tbuf, sums_out, sums_in,
    ra_send, ra_recv, rb_send, rb_recv,
    y_send, y_recv, z_send, z_recv, d_send, d_recv,
    c_send, c_recv, t_send, t_recv, s_send, s_recv,
):
    row, col = lax.axis_index("row"), lax.axis_index("col")
    z, s = row // 2, row % 2
    y, h, c = col // 4, (col // 2) % 2, col % 2
    x = 2 * h + s
    accounts = 8192

    def dev(y_, z_, x_, c_):
        return (2 * z_ + x_ % 2, 4 * y_ + 2 * (x_ // 2) + c_)

    def up(v, d, n):
        return lax.rem(v + (d + n), n)

    def remote(src, dst, send, recv, target):
        return pltpu.make_async_remote_copy(
            src_ref=src, dst_ref=dst, send_sem=send, recv_sem=recv,
            device_id=target, device_id_type=MESH,
        )

    barrier = pltpu.get_barrier_semaphore()
    senders = [
        dev(up(y, 1, 8), z, x, c), dev(up(y, -1, 8), z, x, c),
        dev(y, up(z, 1, 8), x, c), dev(y, up(z, -1, 8), x, c),
        dev(y, z, up(x, 1, 4), c), dev(y, z, up(x, -1, 4), c),
        dev(y, z, x, 1 - c),
        dev(y, z, 2 * h + c, s),
        dev(y, z, h, c), dev(y, z, 2 + h, c),
    ]
    for m in range(8):
        for k in range(2):
            senders.append(dev(z, m, 2 * h + c, k))
            senders.append(dev(z, m, 2 * s + k, y // 4))
    for target in senders:
        pl.semaphore_signal(barrier, inc=1, device_id=target, device_id_type=MESH)
    pl.semaphore_wait(barrier, len(senders))

    a_self = s == c
    a_target = dev(y, z, 2 * h + c, s)

    def lanes(v):
        return pl.ds(pl.multiple_of(v * 256, 256), 256)

    def move_a(p):
        return remote(
            w_ref.at[pl.ds(128 * p, 128), :], a_buf.at[s, p, :, lanes(y)],
            ra_send.at[p], ra_recv.at[p], a_target,
        )

    def move_a_local(p):
        return pltpu.make_async_copy(
            w_ref.at[pl.ds(128 * p, 128), :], a_buf.at[s, p, :, lanes(y)], ra_recv.at[p]
        )

    def arrived_a(p):
        return remote(
            a_buf.at[c, p, :, lanes(y)], a_buf.at[c, p, :, lanes(y)],
            ra_send.at[p], ra_recv.at[p], a_target,
        )

    def rows(v):
        return pl.ds(pl.multiple_of(v * 256, 256), 256)

    def move_b(half, j):
        return remote(
            w_ref.at[pl.ds(256 * half, 256), pl.ds(128 * j, 128)], b_buf.at[h, j, rows(z), :],
            rb_send.at[half, j], rb_recv.at[h, j], dev(y, z, 2 * s + half, c),
        )

    def move_b_local(half, j):
        return pltpu.make_async_copy(
            w_ref.at[pl.ds(256 * half, 256), pl.ds(128 * j, 128)], b_buf.at[h, j, rows(z), :],
            rb_recv.at[h, j],
        )

    def arrived_b(p):
        hh, j = (p + c) % 2, p // 2
        return remote(
            b_buf.at[hh, j, rows(z), :], b_buf.at[hh, j, rows(z), :],
            rb_send.at[0, 0], rb_recv.at[hh, j], a_target,
        )

    for p in range(PHASES):
        @pl.when(a_self)
        def _():
            move_a_local(p).start()

        @pl.when(jnp.logical_not(a_self))
        def _():
            move_a(p).start()

        @pl.when((p + c) % 2 == h)
        def _():
            for half in range(2):
                @pl.when(x == 2 * s + half)
                def _():
                    move_b_local(half, p // 2).start()

                @pl.when(x != 2 * s + half)
                def _():
                    move_b(half, p // 2).start()

    right = (4, 3, 4, 3)

    def hop_a(p, direction, k):
        yy = up(y, -direction * k, 8)
        block = a_buf.at[c, p, :, lanes(yy)]
        return remote(
            block, block, y_send.at[p, (1 - direction) // 2, k], y_recv.at[p, yy],
            dev(up(y, direction, 8), z, x, c),
        )

    def hop_b(p, direction, k):
        zz = up(z, -direction * k, 8)
        block = b_buf.at[(p + c) % 2, p // 2, rows(zz), :]
        return remote(
            block, block, z_send.at[p, (1 - direction) // 2, k], z_recv.at[p, zz],
            dev(y, up(z, direction, 8), x, c),
        )

    def share(p, yy, owner=None):
        block = a_buf.at[c if owner is None else owner, p, :, lanes(yy)]
        return remote(block, block, d_send.at[p, yy], d_recv.at[p, yy], dev(y, z, x, 1 - c))

    def steps(p, direction):
        return right[p] if direction == 1 else 7 - right[p]

    def place(i, p):
        return (p + c) % 2, p // 2, 1 - 2 * ((i + p // 2) % 2)

    def product(i, p):
        hh, j, _ = place(i, p)
        left = a_buf[:, i].reshape(256, 2048)
        value = jnp.dot(left, b_buf[hh, j], preferred_element_type=jnp.float32)
        part[0, hh, i, j] = value[:128]
        part[1, hh, i, j] = value[128:]

    def roles(i, p, k):
        hh, j, way = place(i, p)
        delta = lax.rem(2 * hh + k + 4 - x, 4)
        relay = lax.rem(way + 4, 4)
        far = delta == 2
        passes = delta == relay
        direct = jnp.logical_and(delta % 2 == 1, jnp.logical_not(passes))
        step = jnp.where(far, way, 2 - delta)
        kind = jnp.where(far, 0, (delta + 1) // 2)
        copy = remote(
            part.at[k, hh, i, j], inbox.at[kind, i, j], c_send.at[k, hh, i, j], c_recv.at[kind, i, j],
            dev(y, z, lax.rem(x + step + 4, 4), c),
        )
        return far, passes, direct, copy

    def landed(kind, i, j):
        return remote(
            inbox.at[kind, i, j], inbox.at[kind, i, j], c_send.at[0, 0, i, j], c_recv.at[kind, i, j],
            a_target,
        )

    def tiles(q):
        return [(q, p) for p in range(q + 1)], [(i, q) for i in range(q)]

    def each(q, action):
        @pl.loop(0, q + 1)
        def _(p):
            action(q, p)

        if q:
            @pl.loop(0, q)
            def _(i):
                action(i, q)

    def first(i, p):
        product(i, p)
        for k in range(2):
            far, _, direct, copy = roles(i, p, k)

            @pl.when(jnp.logical_or(far, direct))
            def _():
                copy.start()

    def second(i, p):
        hh, j, _ = place(i, p)
        for k in range(2):
            _, passes, _, copy = roles(i, p, k)

            @pl.when(passes)
            def _():
                landed(0, i, j).wait_recv()
                part[k, hh, i, j] += inbox[0, i, j]
                copy.start()

    def mirror(u, hh):
        src = b_buf.at[hh, :, pl.ds(pl.multiple_of(u * 256 + z * 32, 32), 32), :]
        dst = tbuf.at[c, :, pl.ds(pl.multiple_of(z * 32, 32), 32), :]
        own = (u == y) & (hh == s) & (s == c) & (y == z)
        copy = remote(src, dst, t_send.at[u, hh], t_recv.at[c, z], dev(u, y, 2 * h + hh, s))
        local = pltpu.make_async_copy(src, dst, t_recv.at[c, z])
        return own, copy, local

    for slot in range(2 * PHASES + 3):
        for p in range(PHASES):
            k = slot - 2 * p
            if k == 0:
                arrived_a(p).wait_recv()
                for direction in (1, -1):
                    hop_a(p, direction, 0).start()
                arrived_b(p).wait_recv()
                for direction in (1, -1):
                    hop_b(p, direction, 0).start()
                share(p, y).start()
            elif 1 <= k <= 4:
                for direction in (1, -1):
                    if k <= steps(p, direction):
                        hop_a(p, direction, k).wait_recv()
                        if k < steps(p, direction):
                            hop_a(p, direction, k).start()
                        share(p, up(y, -direction * k, 8)).start()
                    if k <= steps(p, direction):
                        hop_b(p, direction, k).wait_recv()
                        if k < steps(p, direction):
                            hop_b(p, direction, k).start()
        if slot == 2 * PHASES + 2:
            @pl.loop(0, 8)
            def _(u):
                for hh in range(2):
                    own, copy, local = mirror(u, hh)

                    @pl.when(own)
                    def _():
                        local.start()

                    @pl.when(jnp.logical_not(own))
                    def _():
                        copy.start()

        for p in range(PHASES):
            k = slot - 2 * p
            if k == 4:
                for yy in range(8):
                    share(p, yy, 1 - c).wait_recv()
                each(p, first)
            elif k == 5 and p < PHASES - 1:
                each(p, second)
    each(PHASES - 1, second)

    for k in range(2):
        for m in range(8):
            dst = tbuf.at[k, :, pl.ds(32 * m, 32), :]
            remote(dst, dst, t_send.at[0, 0], t_recv.at[k, m], a_target).wait_recv()
    scale = 2.0 / math.sqrt(accounts)
    for j in range(2):
        sums_out[j] = jnp.zeros((1, 128), jnp.float32)
        for i in range(4):
            landed(1, i, j).wait_recv()
            landed(2, i, j).wait_recv()
            paths = part[s, h, i, j] + inbox[1, i, j] + inbox[2, i, j]
            back = tbuf[i // 2, i % 2, pl.ds(128 * j, 128), :].astype(jnp.float32).T
            value = paths * back * scale
            edge_ref[pl.ds(128 * i, 128), pl.ds(128 * j, 128)] = value
            sums_out[j] += jnp.sum(value, axis=0, keepdims=True)

    def deliver(t):
        cc = 16 * c + t
        own = (y == z) & (h == s) & (cc == col)
        copy = remote(
            sums_out.at[t // 8], sums_in.at[row], s_send.at[t], s_recv.at[row], (2 * y + h, cc)
        )
        local = pltpu.make_async_copy(sums_out.at[t // 8], sums_in.at[row], s_recv.at[row])
        return own, copy, local

    for t in range(16):
        own, copy, local = deliver(t)

        @pl.when(own)
        def _():
            local.start()

        @pl.when(jnp.logical_not(own))
        def _():
            copy.start()

    for p in range(PHASES):
        @pl.when(jnp.logical_not(a_self))
        def _():
            move_a(p).wait_send()

        @pl.when((p + c) % 2 == h)
        def _():
            for half in range(2):
                @pl.when(x != 2 * s + half)
                def _():
                    move_b(half, p // 2).wait_send()

        for direction in (1, -1):
            for k in range(steps(p, direction)):
                hop_a(p, direction, k).wait_send()
                hop_b(p, direction, k).wait_send()
        for yy in range(8):
            share(p, yy).wait_send()

        @pl.loop(0, PHASES)
        def _(i):
            for k in range(2):
                far, passes, direct, copy = roles(i, p, k)

                @pl.when(far | passes | direct)
                def _():
                    copy.wait_send()

    @pl.loop(0, 8)
    def _(u):
        for hh in range(2):
            own, copy, _ = mirror(u, hh)

            @pl.when(jnp.logical_not(own))
            def _():
                copy.wait_send()

    total = jnp.zeros((1, 128), jnp.float32)
    for r in range(16):
        remote(sums_in.at[r], sums_in.at[r], s_send.at[r], s_recv.at[r], a_target).wait_recv()
        total = total + sums_in[r]
    total = total * (1.0 / math.sqrt(accounts))
    share_of = pltpu.roll(total, lax.rem(128 - 16 * (col % 8), 128), 1)
    acct_ref[...] = share_of[:, :16]
    for t in range(16):
        own, copy, _ = deliver(t)

        @pl.when(jnp.logical_not(own))
        def _():
            copy.wait_send()


def body(weights):
    dma = pltpu.SemaphoreType.DMA
    edge, acct = pl.pallas_call(
        kernel,
        out_shape=(
            jax.ShapeDtypeStruct((512, 256), jnp.float32),
            jax.ShapeDtypeStruct((1, 16), jnp.float32),
        ),
        in_specs=[pl.BlockSpec(memory_space=pltpu.VMEM)],
        out_specs=(
            pl.BlockSpec(memory_space=pltpu.VMEM),
            pl.BlockSpec(memory_space=pltpu.VMEM),
        ),
        scratch_shapes=[
            pltpu.VMEM((2, 4, 128, 2048), jnp.bfloat16),
            pltpu.VMEM((2, 2, 2048, 128), jnp.bfloat16),
            pltpu.VMEM((2, 2, 4, 2, 128, 128), jnp.float32),
            pltpu.VMEM((3, 4, 2, 128, 128), jnp.float32),
            pltpu.VMEM((2, 2, 256, 128), jnp.bfloat16),
            pltpu.VMEM((2, 1, 128), jnp.float32),
            pltpu.VMEM((16, 1, 128), jnp.float32),
            dma((4,)), dma((4,)), dma((2, 2)), dma((2, 2)),
            dma((4, 2, 4)), dma((4, 8)), dma((4, 2, 4)), dma((4, 8)), dma((4, 8)), dma((4, 8)),
            dma((2, 2, 4, 2)), dma((3, 4, 2)), dma((8, 2)), dma((2, 8)), dma((16,)), dma((16,)),
        ],
        compiler_params=pltpu.CompilerParams(
            collective_id=0, has_side_effects=True, vmem_limit_bytes=32 * 1024 * 1024
        ),
        name="cycles",
    )(weights)
    return edge, acct.reshape(16)


def solution(mesh):
    return jax.shard_map(
        body,
        mesh=mesh,
        in_specs=(P("row", "col"),),
        out_specs=(P("row", "col"), P(("row", "col"))),
        check_vma=False,
    )
```

```python
import math

import jax
import jax.numpy as jnp
from jax import lax
from jax.experimental import pallas as pl
from jax.experimental.pallas import tpu as pltpu
from jax.sharding import PartitionSpec as P

MESH = pl.DeviceIdType.MESH
PHASES = 4
START = (0, 0, 0, 0)


def kernel(
    w_ref, edge_ref, acct_ref,
    a_buf, b_buf, part, inbox, tbuf, sums_out, sums_in,
    ra_send, ra_recv, rb_send, rb_recv,
    y_send, y_recv, z_send, z_recv, d_send, d_recv,
    c_send, c_recv, t_send, t_recv, s_send, s_recv,
):
    row, col = lax.axis_index("row"), lax.axis_index("col")
    z, s = row // 2, row % 2
    y, h, c = col // 4, (col // 2) % 2, col % 2
    x = 2 * h + s
    accounts = 8192

    def dev(y_, z_, x_, c_):
        return (2 * z_ + x_ % 2, 4 * y_ + 2 * (x_ // 2) + c_)

    def up(v, d, n):
        return lax.rem(v + (d + n), n)

    def remote(src, dst, send, recv, target):
        return pltpu.make_async_remote_copy(
            src_ref=src, dst_ref=dst, send_sem=send, recv_sem=recv,
            device_id=target, device_id_type=MESH,
        )

    barrier = pltpu.get_barrier_semaphore()
    senders = [
        dev(up(y, 1, 8), z, x, c), dev(up(y, -1, 8), z, x, c),
        dev(y, up(z, 1, 8), x, c), dev(y, up(z, -1, 8), x, c),
        dev(y, z, up(x, 1, 4), c), dev(y, z, up(x, -1, 4), c),
        dev(y, z, x, 1 - c),
        dev(y, z, 2 * h + c, s),
        dev(y, z, h, c), dev(y, z, 2 + h, c),
    ]
    for k in range(2):
        for q in range(2):
            senders.append(dev(z, (y + z) % 4 + 4 * q, 2 * h + c, k))
        for m in range(8):
            senders.append(dev(z, m, 2 * s + k, y // 4))
    for target in senders:
        pl.semaphore_signal(barrier, inc=1, device_id=target, device_id_type=MESH)
    pl.semaphore_wait(barrier, len(senders))

    a_self = s == c
    a_target = dev(y, z, 2 * h + c, s)

    def lanes(v):
        return pl.ds(pl.multiple_of(v * 256, 256), 256)

    def move_a(p):
        return remote(
            w_ref.at[pl.ds(128 * p, 128), :], a_buf.at[s, p, :, lanes(y)],
            ra_send, ra_recv.at[p], a_target,
        )

    def move_a_local(p):
        return pltpu.make_async_copy(
            w_ref.at[pl.ds(128 * p, 128), :], a_buf.at[s, p, :, lanes(y)], ra_recv.at[p]
        )

    def arrived_a(p):
        return remote(
            a_buf.at[c, p, :, lanes(y)], a_buf.at[c, p, :, lanes(y)],
            ra_send, ra_recv.at[p], a_target,
        )

    def rows(v):
        return pl.ds(pl.multiple_of(v * 256, 256), 256)

    def move_b(half, j):
        return remote(
            w_ref.at[pl.ds(256 * half, 256), pl.ds(128 * j, 128)], b_buf.at[h, j, rows(z), :],
            rb_send.at[half], rb_recv.at[h, j], dev(y, z, 2 * s + half, c),
        )

    def move_b_local(half, j):
        return pltpu.make_async_copy(
            w_ref.at[pl.ds(256 * half, 256), pl.ds(128 * j, 128)], b_buf.at[h, j, rows(z), :],
            rb_recv.at[h, j],
        )

    def arrived_b(p):
        hh, j = (p + c) % 2, p // 2
        return remote(
            b_buf.at[hh, j, rows(z), :], b_buf.at[hh, j, rows(z), :],
            rb_send.at[0], rb_recv.at[hh, j], a_target,
        )

    for p in range(PHASES):
        @pl.when(a_self)
        def _():
            move_a_local(p).start()

        @pl.when(jnp.logical_not(a_self))
        def _():
            move_a(p).start()

        @pl.when((p + c) % 2 == h)
        def _():
            for half in range(2):
                @pl.when(x == 2 * s + half)
                def _():
                    move_b_local(half, p // 2).start()

                @pl.when(x != 2 * s + half)
                def _():
                    move_b(half, p // 2).start()

    right = (4, 3, 4, 3)

    def hop_a(p, direction, k):
        yy = up(y, -direction * k, 8)
        block = a_buf.at[c, p, :, lanes(yy)]
        return remote(
            block, block, y_send, y_recv.at[p, yy],
            dev(up(y, direction, 8), z, x, c),
        )

    def hop_b(p, direction, k):
        zz = up(z, -direction * k, 8)
        block = b_buf.at[(p + c) % 2, p // 2, rows(zz), :]
        return remote(
            block, block, z_send, z_recv.at[p, zz],
            dev(y, up(z, direction, 8), x, c),
        )

    def share(p, yy):
        block = a_buf.at[c, p, :, lanes(yy)]
        return remote(block, block, d_send, d_recv.at[p], dev(y, z, x, 1 - c))

    def shared(p):
        block = a_buf.at[1 - c, p]
        return remote(block, block, d_send, d_recv.at[p], a_target)

    def steps(p, direction):
        return right[p] if direction == 1 else 7 - right[p]

    def place(i, p):
        return (p + c) % 2, p // 2, 1 - 2 * ((i + p // 2) % 2)

    def product(i, p):
        hh, j, _ = place(i, p)
        left = a_buf[:, i].reshape(256, 2048)
        value = jnp.dot(left, b_buf[hh, j], preferred_element_type=jnp.float32)
        part[0, hh, i, j] = value[:128]
        part[1, hh, i, j] = value[128:]

    def roles(i, p, k):
        hh, j, way = place(i, p)
        delta = lax.rem(2 * hh + k + 4 - x, 4)
        relay = lax.rem(way + 4, 4)
        far = delta == 2
        passes = delta == relay
        direct = jnp.logical_and(delta % 2 == 1, jnp.logical_not(passes))
        step = jnp.where(far, way, 2 - delta)
        kind = jnp.where(far, 0, (delta + 1) // 2)
        copy = remote(
            part.at[k, hh, i, j], inbox.at[kind, i, j], c_send, c_recv.at[kind, i, j],
            dev(y, z, lax.rem(x + step + 4, 4), c),
        )
        return far, passes, direct, copy

    def landed(kind, i, j):
        return remote(
            inbox.at[kind, i, j], inbox.at[kind, i, j], c_send, c_recv.at[kind, i, j],
            a_target,
        )

    def tiles(q):
        return [(q, p) for p in range(q + 1)], [(i, q) for i in range(q)]

    def each(q, action):
        @pl.loop(0, q + 1)
        def _(p):
            action(q, p)

        if q:
            @pl.loop(0, q)
            def _(i):
                action(i, q)

    def first(i, p):
        product(i, p)
        for k in range(2):
            far, _, direct, copy = roles(i, p, k)

            @pl.when(jnp.logical_or(far, direct))
            def _():
                copy.start()

    def second(i, p):
        hh, j, _ = place(i, p)
        for k in range(2):
            _, passes, _, copy = roles(i, p, k)

            @pl.when(passes)
            def _():
                landed(0, i, j).wait_recv()
                part[k, hh, i, j] += inbox[0, i, j]
                copy.start()

    def mirror(q, hh):
        u = (z + 8 - y) % 4 + 4 * q
        half = z // 4
        src = b_buf.at[hh, :, pl.ds(pl.multiple_of(u * 256 + half * 128, 128), 128), :]
        dst = tbuf.at[c, :, pl.ds(pl.multiple_of(half * 128, 128), 128), :]
        own = (u == y) & (hh == s) & (s == c) & (y == z)
        copy = remote(src, dst, t_send.at[q, hh], t_recv, dev(u, y, 2 * h + hh, s))
        local = pltpu.make_async_copy(src, dst, t_recv)
        return own, copy, local

    last = max(START) + 4
    for slot in range(last + 1):
        for p in range(PHASES):
            k = slot - START[p]
            if k == 0:
                arrived_a(p).wait_recv()
                for direction in (1, -1):
                    hop_a(p, direction, 0).start()
                arrived_b(p).wait_recv()
                for direction in (1, -1):
                    hop_b(p, direction, 0).start()
                share(p, y).start()
            elif 1 <= k <= 4:
                for direction in (1, -1):
                    if k <= steps(p, direction):
                        hop_a(p, direction, k).wait_recv()
                        if k < steps(p, direction):
                            hop_a(p, direction, k).start()
                        share(p, up(y, -direction * k, 8)).start()
                    if k <= steps(p, direction):
                        hop_b(p, direction, k).wait_recv()
                        if k < steps(p, direction):
                            hop_b(p, direction, k).start()
        if slot == last:
            for q in range(2):
                for hh in range(2):
                    own, copy, local = mirror(q, hh)

                    @pl.when(own)
                    def _():
                        local.start()

                    @pl.when(jnp.logical_not(own))
                    def _():
                        copy.start()

        for p in range(PHASES):
            k = slot - START[p]
            if k == 4:
                shared(p).wait_recv()
                each(p, first)
            elif k == 5:
                each(p, second)
    for p in range(PHASES):
        if START[p] + 5 > last:
            each(p, second)

    remote(tbuf, tbuf, t_send.at[0, 0], t_recv, a_target).wait_recv()
    scale = 2.0 / math.sqrt(accounts)
    for j in range(2):
        for i in range(4):
            back = tbuf[i // 2, i % 2, pl.ds(128 * j, 128), :].astype(jnp.float32).T
            edge_ref[pl.ds(128 * i, 128), pl.ds(128 * j, 128)] = back * scale
    for j in range(2):
        column = jnp.zeros((1, 128), jnp.float32)
        for i in range(4):
            landed(1, i, j).wait_recv()
            landed(2, i, j).wait_recv()
            paths = part[s, h, i, j] + inbox[1, i, j] + inbox[2, i, j]
            here = pl.ds(128 * i, 128), pl.ds(128 * j, 128)
            value = paths * edge_ref[here]
            edge_ref[here] = value
            column += jnp.sum(value, axis=0, keepdims=True)
        sums_out[j] = column

    def deliver(t, which):
        return remote(
            sums_out.at[t // 8], sums_in.at[row], s_send.at[which], s_recv, (2 * y + h, 16 * c + t)
        )

    near = col % 16
    own = (y == z) & (h == s) & (16 * c + near == col)
    for q in range(15):
        deliver((col + 1 + q) % 16, 0).start()

    @pl.when(own)
    def _():
        pltpu.make_async_copy(sums_out.at[near // 8], sums_in.at[row], s_recv).start()

    @pl.when(jnp.logical_not(own))
    def _():
        deliver(near, 1).start()

    def left(ref, send):
        remote(ref, ref, send, d_recv.at[0], a_target).wait_send()

    @pl.when(jnp.logical_not(a_self))
    def _():
        left(w_ref, ra_send)

    for half in range(2):
        @pl.when(x != 2 * s + half)
        def _():
            left(w_ref.at[pl.ds(0, 256), :], rb_send.at[half])

    left(a_buf.at[0, :, :, pl.ds(0, 1792)], y_send)
    left(b_buf.at[:, :, pl.ds(0, 1792), :], z_send)
    left(a_buf.at[0], d_send)
    left(inbox, c_send)
    for q in range(2):
        for hh in range(2):
            mine, copy, _ = mirror(q, hh)

            @pl.when(jnp.logical_not(mine))
            def _():
                copy.wait_send()

    remote(sums_in, sums_in, s_send.at[0], s_recv, a_target).wait_recv()
    total = jnp.sum(sums_in[...], axis=0) * (1.0 / math.sqrt(accounts))
    acct_ref[...] = pltpu.roll(total, lax.rem(128 - 16 * (col % 8), 128), 1)[:, :16]
    left(sums_in.at[pl.ds(0, 15)], s_send.at[0])

    @pl.when(jnp.logical_not(own))
    def _():
        left(sums_in.at[pl.ds(0, 1)], s_send.at[1])


def body(weights):
    dma = pltpu.SemaphoreType.DMA
    edge, acct = pl.pallas_call(
        kernel,
        out_shape=(
            jax.ShapeDtypeStruct((512, 256), jnp.float32),
            jax.ShapeDtypeStruct((1, 16), jnp.float32),
        ),
        in_specs=[pl.BlockSpec(memory_space=pltpu.VMEM)],
        out_specs=(
            pl.BlockSpec(memory_space=pltpu.VMEM),
            pl.BlockSpec(memory_space=pltpu.VMEM),
        ),
        scratch_shapes=[
            pltpu.VMEM((2, 4, 128, 2048), jnp.bfloat16),
            pltpu.VMEM((2, 2, 2048, 128), jnp.bfloat16),
            pltpu.VMEM((2, 2, 4, 2, 128, 128), jnp.float32),
            pltpu.VMEM((3, 4, 2, 128, 128), jnp.float32),
            pltpu.VMEM((2, 2, 256, 128), jnp.bfloat16),
            pltpu.VMEM((2, 1, 128), jnp.float32),
            pltpu.VMEM((16, 1, 128), jnp.float32),
            dma, dma((4,)), dma((2,)), dma((2, 2)),
            dma, dma((4, 8)), dma, dma((4, 8)), dma, dma((4,)),
            dma, dma((3, 4, 2)), dma((2, 2)), dma, dma((2,)), dma,
        ],
        compiler_params=pltpu.CompilerParams(
            collective_id=0, has_side_effects=True, vmem_limit_bytes=32 * 1024 * 1024
        ),
        name="cycles",
    )(weights)
    return edge, acct.reshape(16)


def solution(mesh):
    return jax.shard_map(
        body,
        mesh=mesh,
        in_specs=(P("row", "col"),),
        out_specs=(P("row", "col"), P(("row", "col"))),
        check_vma=False,
    )
```

```python
import math

import jax
import jax.numpy as jnp
from jax import lax
from jax.experimental import pallas as pl
from jax.experimental.pallas import tpu as pltpu
from jax.sharding import PartitionSpec as P

MESH = pl.DeviceIdType.MESH
PHASES = 4
SUBS = 2 * PHASES
START = (0,) * SUBS


def kernel(
    w_ref, edge_ref, acct_ref,
    a_buf, b_buf, part, inbox, tbuf, sums_out, sums_in,
    ra_send, ra_recv, rb_send, rb_recv,
    y_send, y_recv, z_send, z_recv, d_send, d_recv,
    c_send, c_recv, t_send, t_recv, s_send, s_recv, ready,
):
    row, col = lax.axis_index("row"), lax.axis_index("col")
    z, s = row // 2, row % 2
    y, h, c = col // 4, (col // 2) % 2, col % 2
    x = 2 * h + s
    accounts = 8192

    def dev(y_, z_, x_, c_):
        return (2 * z_ + x_ % 2, 4 * y_ + 2 * (x_ // 2) + c_)

    def up(v, d, n):
        return lax.rem(v + (d + n), n)

    def remote(src, dst, send, recv, target):
        return pltpu.make_async_remote_copy(
            src_ref=src, dst_ref=dst, send_sem=send, recv_sem=recv,
            device_id=target, device_id_type=MESH,
        )

    barrier = pltpu.get_barrier_semaphore()
    senders = [
        dev(up(y, 1, 8), z, x, c), dev(up(y, -1, 8), z, x, c),
        dev(y, up(z, 1, 8), x, c), dev(y, up(z, -1, 8), x, c),
        dev(y, z, x, 1 - c),
    ]
    for step in range(1, 4):
        for k in range(2):
            senders.append(dev(y, z, up(x, step, 4), k))
    for target in senders:
        pl.semaphore_signal(barrier, inc=1, device_id=target, device_id_type=MESH)
    pl.semaphore_wait(barrier, len(senders))

    a_self = s == c
    a_target = dev(y, z, 2 * h + c, s)

    def lanes(v):
        return pl.ds(pl.multiple_of(v * 256, 256), 256)

    def rows(v, q):
        return pl.ds(pl.multiple_of(v * 256 + 128 * (q % 2), 128), 128)

    def a_block(owner, q, yy):
        return a_buf.at[owner, q // 2, pl.ds(64 * (q % 2), 64), lanes(yy)]

    def b_block(q, zz):
        p = q // 2
        return b_buf.at[(p + c) % 2, p // 2, rows(zz, q), :]

    def move_a(q):
        return w_ref.at[pl.ds(64 * q, 64), :], a_block(s, q, y), ra_recv.at[q]

    def move_b(half, q):
        src = w_ref.at[pl.ds(256 * half + 128 * (q % 2), 128), pl.ds(128 * (q // 4), 128)]
        return src, b_block(q, z), rb_recv.at[q]

    for q in range(SUBS):
        src, dst, arrived = move_a(q)

        @pl.when(a_self)
        def _():
            pltpu.make_async_copy(src, dst, arrived).start()

        @pl.when(jnp.logical_not(a_self))
        def _():
            remote(src, dst, ra_send, arrived, a_target).start()

        @pl.when((q // 2 + c) % 2 == h)
        def _():
            for half in range(2):
                src, dst, arrived = move_b(half, q)

                @pl.when(x == 2 * s + half)
                def _():
                    pltpu.make_async_copy(src, dst, arrived).start()

                @pl.when(x != 2 * s + half)
                def _():
                    remote(src, dst, rb_send.at[half], arrived, dev(y, z, 2 * s + half, c)).start()

    def hop_a(q, direction, k):
        yy = up(y, -direction * k, 8)
        block = a_block(c, q, yy)
        return remote(block, block, y_send, y_recv.at[q, yy], dev(up(y, direction, 8), z, x, c))

    def hop_b(q, direction, k):
        zz = up(z, -direction * k, 8)
        block = b_block(q, zz)
        return remote(block, block, z_send, z_recv.at[q, zz], dev(y, up(z, direction, 8), x, c))

    def share(q, yy):
        block = a_block(c, q, yy)
        return remote(block, block, d_send, d_recv.at[q // 2], dev(y, z, x, 1 - c))

    def shared(p):
        block = a_buf.at[1 - c, p]
        return remote(block, block, d_send, d_recv.at[p], a_target)

    def steps(q, direction):
        return 3 + (q + (1 + direction) // 2) % 2

    def place(i, p):
        return (p + c) % 2, p // 2, 1 - 2 * ((i + p // 2) % 2)

    def product(i, p):
        hh, j, _ = place(i, p)
        left = a_buf[:, i].reshape(256, 2048)
        value = jnp.dot(left, b_buf[hh, j], preferred_element_type=jnp.float32)
        part[0, hh, i, j] = value[:128]
        part[1, hh, i, j] = value[128:]

    def roles(i, p, k):
        hh, j, way = place(i, p)
        delta = lax.rem(2 * hh + k + 4 - x, 4)
        relay = lax.rem(way + 4, 4)
        far = delta == 2
        passes = delta == relay
        direct = jnp.logical_and(delta % 2 == 1, jnp.logical_not(passes))
        step = jnp.where(far, way, 2 - delta)
        kind = jnp.where(far, 0, (delta + 1) // 2)
        copy = remote(
            part.at[k, hh, i, j], inbox.at[kind, i, j], c_send, c_recv.at[kind, i, j],
            dev(y, z, lax.rem(x + step + 4, 4), c),
        )
        return far, passes, direct, copy

    def landed(kind, i, j):
        return remote(
            inbox.at[kind, i, j], inbox.at[kind, i, j], c_send, c_recv.at[kind, i, j],
            a_target,
        )

    def tiles(q):
        return [(q, p) for p in range(q + 1)], [(i, q) for i in range(q)]

    def each(q, action):
        @pl.loop(0, q + 1)
        def _(p):
            action(q, p)

        if q:
            @pl.loop(0, q)
            def _(i):
                action(i, q)

    def first(i, p):
        product(i, p)
        for k in range(2):
            far, _, direct, copy = roles(i, p, k)

            @pl.when(jnp.logical_or(far, direct))
            def _():
                copy.start()

    def second(i, p):
        hh, j, _ = place(i, p)
        for k in range(2):
            _, passes, _, copy = roles(i, p, k)

            @pl.when(passes)
            def _():
                landed(0, i, j).wait_recv()
                part[k, hh, i, j] += inbox[0, i, j]
                copy.start()

    def mirror(q, hh):
        u = (z + 8 - y) % 4 + 4 * q
        half = z // 4
        src = b_buf.at[hh, :, pl.ds(pl.multiple_of(u * 256 + half * 128, 128), 128), :]
        dst = tbuf.at[c, :, pl.ds(pl.multiple_of(half * 128, 128), 128), :]
        own = (u == y) & (hh == s) & (s == c) & (y == z)
        copy = remote(src, dst, t_send.at[q, hh], t_recv, dev(u, y, 2 * h + hh, s))
        local = pltpu.make_async_copy(src, dst, t_recv)
        return own, copy, local

    ends = [max(START[2 * p], START[2 * p + 1]) + 4 for p in range(PHASES)]
    last = max(ends)
    for slot in range(last + 1):
        for q in range(SUBS):
            k = slot - START[q]
            if k == 0:
                block = a_block(c, q, y)
                remote(block, block, ra_send, ra_recv.at[q], a_target).wait_recv()
                for direction in (1, -1):
                    hop_a(q, direction, 0).start()
                block = b_block(q, z)
                remote(block, block, ra_send, rb_recv.at[q], a_target).wait_recv()
                for direction in (1, -1):
                    hop_b(q, direction, 0).start()
                share(q, y).start()
            elif 1 <= k <= 4:
                for direction in (1, -1):
                    if k <= steps(q, direction):
                        hop_a(q, direction, k).wait_recv()
                        if k < steps(q, direction):
                            hop_a(q, direction, k).start()
                        hop_b(q, direction, k).wait_recv()
                        if k < steps(q, direction):
                            hop_b(q, direction, k).start()
                        share(q, up(y, -direction * k, 8)).start()
        if slot == START[0] + 4:
            for k in range(1, 8):
                pl.semaphore_signal(
                    ready, inc=1, device_id=dev(up(y, k, 8), z, x, c), device_id_type=MESH
                )
        for p in range(PHASES):
            if slot == ends[p]:
                shared(p).wait_recv()
                each(p, first)
            elif slot == ends[p] + 1:
                each(p, second)
    pl.semaphore_wait(ready, 7)
    for q in range(2):
        for hh in range(2):
            mine, copy, local = mirror(q, hh)

            @pl.when(mine)
            def _():
                local.start()

            @pl.when(jnp.logical_not(mine))
            def _():
                copy.start()

    for p in range(PHASES):
        if ends[p] == last:
            each(p, second)

    remote(tbuf, tbuf, t_send.at[0, 0], t_recv, a_target).wait_recv()
    scale = 2.0 / math.sqrt(accounts)
    for j in range(2):
        for i in range(4):
            back = tbuf[i // 2, i % 2, pl.ds(128 * j, 128), :].astype(jnp.float32).T
            edge_ref[pl.ds(128 * i, 128), pl.ds(128 * j, 128)] = back * scale
    for i in range(4):
        both = jnp.zeros((128, 128), jnp.float32)
        for j in range(2):
            landed(1, i, j).wait_recv()
            landed(2, i, j).wait_recv()
            paths = part[s, h, i, j] + inbox[1, i, j] + inbox[2, i, j]
            here = pl.ds(128 * i, 128), pl.ds(128 * j, 128)
            value = paths * edge_ref[here]
            edge_ref[here] = value
            both += value
        sums_out[i] = jnp.sum(both.T, axis=0, keepdims=True)

    for q in range(31):
        t = (col + 1 + q) % 32
        remote(sums_out.at[t // 8], sums_in.at[col], s_send, s_recv, (row, t)).start()
    sums_in[col] = sums_out[col // 8]

    def left(ref, send):
        remote(ref, ref, send, d_recv.at[0], a_target).wait_send()

    @pl.when(jnp.logical_not(a_self))
    def _():
        left(w_ref, ra_send)

    for half in range(2):
        @pl.when(x != 2 * s + half)
        def _():
            left(w_ref.at[pl.ds(0, 256), :], rb_send.at[half])

    left(a_buf.at[0, :, :, pl.ds(0, 1792)], y_send)
    left(b_buf.at[:, :, pl.ds(0, 1792), :], z_send)
    left(a_buf.at[0], d_send)
    left(inbox, c_send)
    for q in range(2):
        for hh in range(2):
            mine, copy, _ = mirror(q, hh)

            @pl.when(jnp.logical_not(mine))
            def _():
                copy.wait_send()

    others = sums_in.at[pl.ds(0, 31)]
    remote(others, others, s_send, s_recv, a_target).wait_recv()
    total = jnp.sum(sums_in[...], axis=0) * (1.0 / math.sqrt(accounts))
    acct_ref[...] = pltpu.roll(total, lax.rem(128 - 16 * (col % 8), 128), 1)[:, :16]
    left(others, s_send)


def body(weights):
    dma = pltpu.SemaphoreType.DMA
    edge, acct = pl.pallas_call(
        kernel,
        out_shape=(
            jax.ShapeDtypeStruct((512, 256), jnp.float32),
            jax.ShapeDtypeStruct((1, 16), jnp.float32),
        ),
        in_specs=[pl.BlockSpec(memory_space=pltpu.VMEM)],
        out_specs=(
            pl.BlockSpec(memory_space=pltpu.VMEM),
            pl.BlockSpec(memory_space=pltpu.VMEM),
        ),
        scratch_shapes=[
            pltpu.VMEM((2, 4, 128, 2048), jnp.bfloat16),
            pltpu.VMEM((2, 2, 2048, 128), jnp.bfloat16),
            pltpu.VMEM((2, 2, 4, 2, 128, 128), jnp.float32),
            pltpu.VMEM((3, 4, 2, 128, 128), jnp.float32),
            pltpu.VMEM((2, 2, 256, 128), jnp.bfloat16),
            pltpu.VMEM((4, 1, 128), jnp.float32),
            pltpu.VMEM((32, 1, 128), jnp.float32),
            dma, dma((8,)), dma((2,)), dma((8,)),
            dma, dma((8, 8)), dma, dma((8, 8)), dma, dma((4,)),
            dma, dma((3, 4, 2)), dma((2, 2)), dma, dma, dma, pltpu.SemaphoreType.REGULAR,
        ],
        compiler_params=pltpu.CompilerParams(
            collective_id=0, has_side_effects=True, vmem_limit_bytes=32 * 1024 * 1024
        ),
        name="cycles",
    )(weights)
    return edge, acct.reshape(16)


def solution(mesh):
    return jax.shard_map(
        body,
        mesh=mesh,
        in_specs=(P("row", "col"),),
        out_specs=(P("row", "col"), P(("row", "col"))),
        check_vma=False,
    )
```

```python
import math

import jax
import jax.numpy as jnp
from jax import lax
from jax.experimental import pallas as pl
from jax.experimental.pallas import tpu as pltpu
from jax.sharding import PartitionSpec as P

MESH = pl.DeviceIdType.MESH
PHASES = 4
SUBS = 2 * PHASES
STEPS = 4


def kernel(
    w_ref, edge_ref, acct_ref,
    a_buf, b_buf, part, inbox, tbuf, sums_out, sums_in,
    ra_send, ra_recv, rb_send, rb_recv,
    y_send, y_recv, z_send, z_recv, d_send, d_recv,
    c_send, c_recv, t_send, t_recv, s_send, s_recv, ready,
):
    row, col = lax.axis_index("row"), lax.axis_index("col")
    z, s = row // 2, row % 2
    y, h, c = col // 4, (col // 2) % 2, col % 2
    x = 2 * h + s
    accounts = 8192

    def dev(y_, z_, x_, c_):
        return (2 * z_ + x_ % 2, 4 * y_ + 2 * (x_ // 2) + c_)

    def up(v, d, n):
        return lax.rem(v + (d + n), n)

    def remote(src, dst, send, recv, target):
        return pltpu.make_async_remote_copy(
            src_ref=src, dst_ref=dst, send_sem=send, recv_sem=recv,
            device_id=target, device_id_type=MESH,
        )

    barrier = pltpu.get_barrier_semaphore()
    senders = [
        dev(up(y, 1, 8), z, x, c), dev(up(y, -1, 8), z, x, c),
        dev(y, up(z, 1, 8), x, c), dev(y, up(z, -1, 8), x, c),
        dev(y, z, x, 1 - c),
    ]
    for step in range(1, 4):
        for k in range(2):
            senders.append(dev(y, z, up(x, step, 4), k))
    for target in senders:
        pl.semaphore_signal(barrier, inc=1, device_id=target, device_id_type=MESH)
    pl.semaphore_wait(barrier, len(senders))

    a_self = s == c
    a_target = dev(y, z, 2 * h + c, s)

    def lanes(v):
        return pl.ds(pl.multiple_of(v * 256, 256), 256)

    def rows(v, q):
        return pl.ds(pl.multiple_of(v * 256 + 128 * (q % 2), 128), 128)

    def a_block(owner, q, yy):
        return a_buf.at[owner, q // 2, pl.ds(64 * (q % 2), 64), lanes(yy)]

    def b_block(q, zz):
        p = q // 2
        return b_buf.at[(p + c) % 2, p // 2, rows(zz, q), :]

    def move_a(q):
        return w_ref.at[pl.ds(64 * q, 64), :], a_block(s, q, y), ra_recv.at[q]

    def move_b(half, q):
        src = w_ref.at[pl.ds(256 * half + 128 * (q % 2), 128), pl.ds(128 * (q // 4), 128)]
        return src, b_block(q, z), rb_recv.at[q]

    for q in range(SUBS):
        src, dst, arrived = move_a(q)

        @pl.when(a_self)
        def _():
            pltpu.make_async_copy(src, dst, arrived).start()

        @pl.when(jnp.logical_not(a_self))
        def _():
            remote(src, dst, ra_send, arrived, a_target).start()

        @pl.when((q // 2 + c) % 2 == h)
        def _():
            for half in range(2):
                src, dst, arrived = move_b(half, q)

                @pl.when(x == 2 * s + half)
                def _():
                    pltpu.make_async_copy(src, dst, arrived).start()

                @pl.when(x != 2 * s + half)
                def _():
                    remote(src, dst, rb_send.at[half], arrived, dev(y, z, 2 * s + half, c)).start()

    def hop_a(q, direction, k):
        yy = up(y, -direction * k, 8)
        block = a_block(c, q, yy)
        return remote(block, block, y_send, y_recv.at[q, yy], dev(up(y, direction, 8), z, x, c))

    def hop_b(q, direction, k):
        zz = up(z, -direction * k, 8)
        block = b_block(q, zz)
        return remote(block, block, z_send, z_recv.at[q, zz], dev(y, up(z, direction, 8), x, c))

    def share(q, yy):
        block = a_block(c, q, yy)
        return remote(block, block, d_send, d_recv.at[q // 2], dev(y, z, x, 1 - c))

    def shared(p):
        block = a_buf.at[1 - c, p]
        return remote(block, block, d_send, d_recv.at[p], a_target)

    def steps(q, direction):
        return 3 + (q + (1 + direction) // 2) % 2

    def product(i, hh):
        left = a_buf[:, i].reshape(256, 2048)
        right = jnp.concatenate([b_buf[hh, 0], b_buf[hh, 1]], axis=1)
        value = jnp.dot(left, right, preferred_element_type=jnp.float32)
        for k in range(2):
            for j in range(2):
                part[k, hh, i, j] = value[128 * k : 128 * k + 128, 128 * j : 128 * j + 128]

    def roles(i, hh, j, k):
        way = 1 - 2 * ((i + j) % 2)
        delta = lax.rem(2 * hh + k + 4 - x, 4)
        far, passes = delta == 2, delta == lax.rem(way + 4, 4)
        direct = jnp.logical_and(delta % 2 == 1, jnp.logical_not(passes))
        step = jnp.where(far, way, 2 - delta)
        kind = jnp.where(far, 0, (delta + 1) // 2)
        copy = remote(
            part.at[k, hh, i, j], inbox.at[kind, i, j], c_send, c_recv.at[kind, i, j],
            dev(y, z, lax.rem(x + step + 4, 4), c),
        )
        return far, passes, direct, copy

    def landed(kind, i, j):
        block = inbox.at[kind, i, j]
        return remote(block, block, c_send, c_recv.at[kind, i, j], a_target)

    def first(i, hh):
        product(i, hh)
        for j in range(2):
            for k in range(2):
                far, _, direct, copy = roles(i, hh, j, k)
                pl.when(jnp.logical_or(far, direct))(copy.start)

    def second(i, hh):
        for j in range(2):
            for k in range(2):
                _, passes, _, copy = roles(i, hh, j, k)

                @pl.when(passes)
                def _():
                    landed(0, i, j).wait_recv()
                    part[k, hh, i, j] += inbox[0, i, j]
                    copy.start()

    def mirror(q, hh):
        u = (z + 8 - y) % 4 + 4 * q
        half = z // 4
        src = b_buf.at[hh, :, pl.ds(pl.multiple_of(u * 256 + half * 128, 128), 128), :]
        dst = tbuf.at[c, :, pl.ds(pl.multiple_of(half * 128, 128), 128), :]
        own = (u == y) & (hh == s) & (s == c) & (y == z)
        copy = remote(src, dst, t_send.at[q, hh], t_recv, dev(u, y, 2 * h + hh, s))
        local = pltpu.make_async_copy(src, dst, t_recv)
        return own, copy, local

    for q in range(SUBS):
        block = a_block(c, q, y)
        remote(block, block, ra_send, ra_recv.at[q], a_target).wait_recv()
        for direction in (1, -1):
            hop_a(q, direction, 0).start()
        block = b_block(q, z)
        remote(block, block, ra_send, rb_recv.at[q], a_target).wait_recv()
        for direction in (1, -1):
            hop_b(q, direction, 0).start()
        share(q, y).start()
    for k in range(1, STEPS + 1):
        for q in range(SUBS):
            for direction in (1, -1):
                if k <= steps(q, direction):
                    hop_a(q, direction, k).wait_recv()
                    if k < steps(q, direction):
                        hop_a(q, direction, k).start()
                    share(q, up(y, -direction * k, 8)).start()
                    hop_b(q, direction, k).wait_recv()
                    if k < steps(q, direction):
                        hop_b(q, direction, k).start()
    for k in range(1, 8):
        pl.semaphore_signal(
            ready, inc=1, device_id=dev(up(y, k, 8), z, x, c), device_id_type=MESH
        )

    @pl.loop(0, PHASES)
    def _(i):
        shared(i).wait_recv()
        first(i, 0)
        first(i, 1)

    pl.semaphore_wait(ready, 7)
    for q in range(2):
        for hh in range(2):
            mine, copy, local = mirror(q, hh)
            pl.when(mine)(local.start)
            pl.when(jnp.logical_not(mine))(copy.start)

    @pl.loop(0, PHASES)
    def _(i):
        second(i, 0)
        second(i, 1)

    remote(tbuf, tbuf, t_send.at[0, 0], t_recv, a_target).wait_recv()
    scale = 2.0 / math.sqrt(accounts)
    for j in range(2):
        for i in range(4):
            back = tbuf[i // 2, i % 2, pl.ds(128 * j, 128), :].astype(jnp.float32).T
            edge_ref[pl.ds(128 * i, 128), pl.ds(128 * j, 128)] = back * scale
    for i in range(4):
        both = jnp.zeros((128, 128), jnp.float32)
        for j in range(2):
            landed(1, i, j).wait_recv()
            landed(2, i, j).wait_recv()
            paths = part[s, h, i, j] + inbox[1, i, j] + inbox[2, i, j]
            here = pl.ds(128 * i, 128), pl.ds(128 * j, 128)
            value = paths * edge_ref[here]
            edge_ref[here] = value
            both += value
        sums_out[i] = jnp.sum(both.T, axis=0, keepdims=True)
        for k in range(1, 9):
            t = 8 * i + (col + k) % 8
            copy = remote(sums_out.at[i], sums_in.at[col], s_send, s_recv, (row, t))
            if k < 8:
                copy.start()
            else:
                pl.when(t != col)(copy.start)
    sums_in[col] = sums_out[col // 8]

    def left(ref, send):
        remote(ref, ref, send, d_recv.at[0], a_target).wait_send()

    @pl.when(jnp.logical_not(a_self))
    def _():
        left(w_ref, ra_send)

    for half in range(2):
        @pl.when(x != 2 * s + half)
        def _():
            left(w_ref.at[pl.ds(0, 256), :], rb_send.at[half])

    left(a_buf.at[0, :, :, pl.ds(0, 1792)], y_send)
    left(b_buf.at[:, :, pl.ds(0, 1792), :], z_send)
    left(a_buf.at[0], d_send)
    left(inbox, c_send)
    for q in range(2):
        for hh in range(2):
            mine, copy, _ = mirror(q, hh)

            @pl.when(jnp.logical_not(mine))
            def _():
                copy.wait_send()

    others = sums_in.at[pl.ds(0, 31)]
    remote(others, others, s_send, s_recv, a_target).wait_recv()
    total = jnp.sum(sums_in[...], axis=0) * (1.0 / math.sqrt(accounts))
    acct_ref[...] = pltpu.roll(total, lax.rem(128 - 16 * (col % 8), 128), 1)[:, :16]
    left(others, s_send)


def body(weights):
    dma = pltpu.SemaphoreType.DMA
    edge, acct = pl.pallas_call(
        kernel,
        out_shape=(
            jax.ShapeDtypeStruct((512, 256), jnp.float32),
            jax.ShapeDtypeStruct((1, 16), jnp.float32),
        ),
        in_specs=[pl.BlockSpec(memory_space=pltpu.VMEM)],
        out_specs=(
            pl.BlockSpec(memory_space=pltpu.VMEM),
            pl.BlockSpec(memory_space=pltpu.VMEM),
        ),
        scratch_shapes=[
            pltpu.VMEM((2, 4, 128, 2048), jnp.bfloat16),
            pltpu.VMEM((2, 2, 2048, 128), jnp.bfloat16),
            pltpu.VMEM((2, 2, 4, 2, 128, 128), jnp.float32),
            pltpu.VMEM((3, 4, 2, 128, 128), jnp.float32),
            pltpu.VMEM((2, 2, 256, 128), jnp.bfloat16),
            pltpu.VMEM((4, 1, 128), jnp.float32),
            pltpu.VMEM((32, 1, 128), jnp.float32),
            dma, dma((8,)), dma((2,)), dma((8,)),
            dma, dma((8, 8)), dma, dma((8, 8)), dma, dma((4,)),
            dma, dma((3, 4, 2)), dma((2, 2)), dma, dma, dma, pltpu.SemaphoreType.REGULAR,
        ],
        compiler_params=pltpu.CompilerParams(
            collective_id=0, has_side_effects=True, vmem_limit_bytes=32 * 1024 * 1024
        ),
        name="cycles",
    )(weights)
    return edge, acct.reshape(16)


def solution(mesh):
    return jax.shard_map(
        body,
        mesh=mesh,
        in_specs=(P("row", "col"),),
        out_specs=(P("row", "col"), P(("row", "col"))),
        check_vma=False,
    )
```

```python
import math

import jax
import jax.numpy as jnp
from jax import lax
from jax.experimental import pallas as pl
from jax.experimental.pallas import tpu as pltpu
from jax.sharding import PartitionSpec as P

MESH = pl.DeviceIdType.MESH
PHASES = 4
SUBS = 2 * PHASES
STEPS = 4


def kernel(
    w_ref, edge_ref, acct_ref,
    a_buf, b_buf, part, inbox, tbuf, sums_out, sums_in,
    ra_send, ra_recv, rb_send, rb_recv,
    y_send, y_recv, z_send, z_recv, d_send, d_recv,
    c_send, c_recv, t_send, t_recv, s_send, s_recv, ready,
):
    row, col = lax.axis_index("row"), lax.axis_index("col")
    z, s = row // 2, row % 2
    y, h, c = col // 4, (col // 2) % 2, col % 2
    x = 2 * h + s
    accounts = 8192

    def dev(y_, z_, x_, c_):
        return (2 * z_ + x_ % 2, 4 * y_ + 2 * (x_ // 2) + c_)

    def up(v, d, n):
        return lax.rem(v + (d + n), n)

    def remote(src, dst, send, recv, target):
        return pltpu.make_async_remote_copy(
            src_ref=src, dst_ref=dst, send_sem=send, recv_sem=recv,
            device_id=target, device_id_type=MESH,
        )

    barrier = pltpu.get_barrier_semaphore()
    senders = [
        dev(up(y, 1, 8), z, x, c), dev(up(y, -1, 8), z, x, c),
        dev(y, up(z, 1, 8), x, c), dev(y, up(z, -1, 8), x, c),
        dev(y, z, x, 1 - c),
    ]
    for step in range(1, 4):
        for k in range(2):
            senders.append(dev(y, z, up(x, step, 4), k))
    for target in senders:
        pl.semaphore_signal(barrier, inc=1, device_id=target, device_id_type=MESH)
    pl.semaphore_wait(barrier, len(senders))

    a_self = s == c
    a_target = dev(y, z, 2 * h + c, s)

    def lanes(v):
        return pl.ds(pl.multiple_of(v * 256, 256), 256)

    def rows(v, q):
        return pl.ds(pl.multiple_of(v * 256 + 128 * (q % 2), 128), 128)

    def a_block(owner, q, yy):
        return a_buf.at[owner, q // 2, pl.ds(64 * (q % 2), 64), lanes(yy)]

    def b_block(q, zz):
        p = q // 2
        return b_buf.at[(p + c) % 2, p // 2, rows(zz, q), :]

    def move_a(q):
        return w_ref.at[pl.ds(64 * q, 64), :], a_block(s, q, y), ra_recv.at[q]

    def move_b(half, q):
        src = w_ref.at[pl.ds(256 * half + 128 * (q % 2), 128), pl.ds(128 * (q // 4), 128)]
        return src, b_block(q, z), rb_recv.at[q]

    for q in range(SUBS):
        src, dst, arrived = move_a(q)

        @pl.when(a_self)
        def _():
            pltpu.make_async_copy(src, dst, arrived).start()

        @pl.when(jnp.logical_not(a_self))
        def _():
            remote(src, dst, ra_send, arrived, a_target).start()

        @pl.when((q // 2 + c) % 2 == h)
        def _():
            for half in range(2):
                src, dst, arrived = move_b(half, q)

                @pl.when(x == 2 * s + half)
                def _():
                    pltpu.make_async_copy(src, dst, arrived).start()

                @pl.when(x != 2 * s + half)
                def _():
                    remote(src, dst, rb_send.at[half], arrived, dev(y, z, 2 * s + half, c)).start()

    def hop_a(q, direction, k):
        yy = up(y, -direction * k, 8)
        block = a_block(c, q, yy)
        return remote(block, block, y_send, y_recv.at[q, yy], dev(up(y, direction, 8), z, x, c))

    def hop_b(q, direction, k):
        zz = up(z, -direction * k, 8)
        block = b_block(q, zz)
        return remote(block, block, z_send, z_recv.at[q, zz], dev(y, up(z, direction, 8), x, c))

    def share(q, yy):
        block = a_block(c, q, yy)
        return remote(block, block, d_send, d_recv.at[q // 2], dev(y, z, x, 1 - c))

    def shared(p):
        block = a_buf.at[1 - c, p]
        return remote(block, block, d_send, d_recv.at[p], a_target)

    def steps(q, direction):
        return 3 + (q + (1 + direction) // 2) % 2

    def product(i, hh):
        left = a_buf[:, i].reshape(256, 2048)
        right = jnp.concatenate([b_buf[hh, 0], b_buf[hh, 1]], axis=1)
        value = jnp.dot(left, right, preferred_element_type=jnp.float32)
        for k in range(2):
            for j in range(2):
                part[k, hh, i, j] = value[128 * k : 128 * k + 128, 128 * j : 128 * j + 128]

    def roles(i, hh, j, k):
        way = 1 - 2 * ((i + j) % 2)
        delta = lax.rem(2 * hh + k + 4 - x, 4)
        far, passes = delta == 2, delta == lax.rem(way + 4, 4)
        direct = jnp.logical_and(delta % 2 == 1, jnp.logical_not(passes))
        step = jnp.where(far, way, 2 - delta)
        kind = jnp.where(far, 0, (delta + 1) // 2)
        copy = remote(
            part.at[k, hh, i, j], inbox.at[kind, i, j], c_send, c_recv.at[kind, i, j],
            dev(y, z, lax.rem(x + step + 4, 4), c),
        )
        return far, passes, direct, copy

    def landed(kind, i, j):
        block = inbox.at[kind, i, j]
        return remote(block, block, c_send, c_recv.at[kind, i, j], a_target)

    def first(i, hh):
        product(i, hh)
        for turn in (0, 2):
            for j in range(2):
                for k in range(2):
                    copies = roles(i, hh, j, k)
                    pl.when(copies[turn])(copies[3].start)

    def second(i, hh):
        for j in range(2):
            for k in range(2):
                _, passes, _, copy = roles(i, hh, j, k)

                @pl.when(passes)
                def _():
                    landed(0, i, j).wait_recv()
                    part[k, hh, i, j] += inbox[0, i, j]
                    copy.start()

    def mirror(q, hh):
        u = (z + 8 - y) % 4 + 4 * q
        half = z // 4
        src = b_buf.at[hh, :, pl.ds(pl.multiple_of(u * 256 + half * 128, 128), 128), :]
        dst = tbuf.at[c, :, pl.ds(pl.multiple_of(half * 128, 128), 128), :]
        own = (u == y) & (hh == s) & (s == c) & (y == z)
        copy = remote(src, dst, t_send.at[q, hh], t_recv, dev(u, y, 2 * h + hh, s))
        local = pltpu.make_async_copy(src, dst, t_recv)
        return own, copy, local

    for q in range(SUBS):
        block = a_block(c, q, y)
        remote(block, block, ra_send, ra_recv.at[q], a_target).wait_recv()
        for direction in (1, -1):
            hop_a(q, direction, 0).start()
        block = b_block(q, z)
        remote(block, block, ra_send, rb_recv.at[q], a_target).wait_recv()
        for direction in (1, -1):
            hop_b(q, direction, 0).start()
        share(q, y).start()
    for k in range(1, STEPS + 1):
        for q in range(SUBS):
            for direction in (1, -1):
                if k <= steps(q, direction):
                    hop_a(q, direction, k).wait_recv()
                    if k < steps(q, direction):
                        hop_a(q, direction, k).start()
                    share(q, up(y, -direction * k, 8)).start()
                    hop_b(q, direction, k).wait_recv()
                    if k < steps(q, direction):
                        hop_b(q, direction, k).start()
    for k in range(1, 8):
        pl.semaphore_signal(
            ready, inc=1, device_id=dev(up(y, k, 8), z, x, c), device_id_type=MESH
        )

    @pl.loop(0, PHASES)
    def _(i):
        shared(i).wait_recv()
        first(i, 0)
        first(i, 1)

    pl.semaphore_wait(ready, 7)
    for q in range(2):
        for hh in range(2):
            mine, copy, local = mirror(q, hh)
            pl.when(mine)(local.start)
            pl.when(jnp.logical_not(mine))(copy.start)

    @pl.loop(0, PHASES)
    def _(i):
        second(i, 0)
        second(i, 1)

    remote(tbuf, tbuf, t_send.at[0, 0], t_recv, a_target).wait_recv()
    scale = 2.0 / math.sqrt(accounts)
    for j in range(2):
        for i in range(4):
            back = tbuf[i // 2, i % 2, pl.ds(128 * j, 128), :].astype(jnp.float32).T
            edge_ref[pl.ds(128 * i, 128), pl.ds(128 * j, 128)] = back * scale
    for i in range(4):
        both = jnp.zeros((128, 128), jnp.float32)
        for j in range(2):
            landed(1, i, j).wait_recv()
            landed(2, i, j).wait_recv()
            paths = part[s, h, i, j] + inbox[1, i, j] + inbox[2, i, j]
            here = pl.ds(128 * i, 128), pl.ds(128 * j, 128)
            value = paths * edge_ref[here]
            edge_ref[here] = value
            both += value
        sums_out[i] = jnp.sum(both.T, axis=0, keepdims=True)
        for k in range(1, 9):
            t = 8 * i + (col + k) % 8
            copy = remote(sums_out.at[i], sums_in.at[col], s_send, s_recv, (row, t))
            if k < 8:
                copy.start()
            else:
                pl.when(t != col)(copy.start)
    sums_in[col] = sums_out[col // 8]

    def left(ref, send):
        remote(ref, ref, send, d_recv.at[0], a_target).wait_send()

    @pl.when(jnp.logical_not(a_self))
    def _():
        left(w_ref, ra_send)

    for half in range(2):
        @pl.when(x != 2 * s + half)
        def _():
            left(w_ref.at[pl.ds(0, 256), :], rb_send.at[half])

    left(a_buf.at[0, :, :, pl.ds(0, 1792)], y_send)
    left(b_buf.at[:, :, pl.ds(0, 1792), :], z_send)
    left(a_buf.at[0], d_send)
    left(inbox, c_send)
    for q in range(2):
        for hh in range(2):
            mine, copy, _ = mirror(q, hh)

            @pl.when(jnp.logical_not(mine))
            def _():
                copy.wait_send()

    others = sums_in.at[pl.ds(0, 31)]
    remote(others, others, s_send, s_recv, a_target).wait_recv()
    total = jnp.sum(sums_in[...], axis=0) * (1.0 / math.sqrt(accounts))
    acct_ref[...] = pltpu.roll(total, lax.rem(128 - 16 * (col % 8), 128), 1)[:, :16]
    left(others, s_send)


def body(weights):
    dma = pltpu.SemaphoreType.DMA
    edge, acct = pl.pallas_call(
        kernel,
        out_shape=(
            jax.ShapeDtypeStruct((512, 256), jnp.float32),
            jax.ShapeDtypeStruct((1, 16), jnp.float32),
        ),
        in_specs=[pl.BlockSpec(memory_space=pltpu.VMEM)],
        out_specs=(
            pl.BlockSpec(memory_space=pltpu.VMEM),
            pl.BlockSpec(memory_space=pltpu.VMEM),
        ),
        scratch_shapes=[
            pltpu.VMEM((2, 4, 128, 2048), jnp.bfloat16),
            pltpu.VMEM((2, 2, 2048, 128), jnp.bfloat16),
            pltpu.VMEM((2, 2, 4, 2, 128, 128), jnp.float32),
            pltpu.VMEM((3, 4, 2, 128, 128), jnp.float32),
            pltpu.VMEM((2, 2, 256, 128), jnp.bfloat16),
            pltpu.VMEM((4, 1, 128), jnp.float32),
            pltpu.VMEM((32, 1, 128), jnp.float32),
            dma, dma((8,)), dma((2,)), dma((8,)),
            dma, dma((8, 8)), dma, dma((8, 8)), dma, dma((4,)),
            dma, dma((3, 4, 2)), dma((2, 2)), dma, dma, dma, pltpu.SemaphoreType.REGULAR,
        ],
        compiler_params=pltpu.CompilerParams(
            collective_id=0, has_side_effects=True, vmem_limit_bytes=32 * 1024 * 1024
        ),
        name="cycles",
    )(weights)
    return edge, acct.reshape(16)


def solution(mesh):
    return jax.shard_map(
        body,
        mesh=mesh,
        in_specs=(P("row", "col"),),
        out_specs=(P("row", "col"), P(("row", "col"))),
        check_vma=False,
    )
```
